768 devices in a mesh: blk: 32 (over z_hi, y, core), uly: 24 (over x, z_lo).
Axes of the slice: x: 4, y: 8, z: 12 (z_hi: 2, z_lo: 6; z = z_hi * 6 + z_lo), core: 2. Of those that a mesh axis runs over, the one named last changes fastest.
Arguments:
- qkv: bfloat16 [49152, 3, 3072], P(('blk', 'uly')), may hold values from -9 to 9
Outputs:
- attended: float32 [49152, 3072], P('blk', 'uly')
- log_total: float32 [24, 49152], P('uly', 'blk')
The draws below stay inside these ranges and needn't reach their ends.
All inputs are finite; a program needn't handle non-finite values.
Results may differ from the reference program's by a relative error of at most 0.0027.
Values may be sent and summed in bfloat16 or wider, within the bound.
A program may use at most 32 MiB of HBM per device.

```python
import math
import jax
import jax.numpy as jnp
from jax import lax

HEADS = 24
HEAD_DIM = 128
TOKENS = 49152
N_BLK = 32


def draw_qkv(key, part):
    first = jax.random.fold_in(jax.random.fold_in(key, 11), 0)
    width = HEADS * HEAD_DIM
    values = jnp.clip(jax.random.normal(first, (TOKENS, 3, width), jnp.float32), -6.0, 6.0)
    return values.astype(jnp.bfloat16)


def setup_inputs(seed: int = 0) -> dict:
    streams_of = jax.random.split(jax.random.key(seed), 2)
    return {
        "qkv": draw_qkv(jax.random.fold_in(streams_of[1], 71), 0),
    }


def block_scores(query_rows, key_rows, temper):
    return jnp.einsum('rhd,khd->hrk', query_rows, key_rows) * temper

def rounded(weights):
    return lax.optimization_barrier(weights.astype(jnp.bfloat16)).astype(jnp.float32)

def reference(qkv):
    block_len = TOKENS // N_BLK
    temper = 1.0 / math.sqrt(HEAD_DIM)
    shaped = qkv.reshape(N_BLK, block_len, 3, HEADS, HEAD_DIM)
    earlier = jnp.roll(shaped[:, :, 1:], 1, axis=0)

    def per_block(pieces):
        current, before = pieces
        current = current.astype(jnp.float32)
        before = before.astype(jnp.float32)
        queries = current[:, 0]
        scores = block_scores(queries, current[:, 1], temper)
        top = lax.optimization_barrier(jnp.max(scores, axis=2))
        weights = jnp.exp(scores - top[:, :, None])
        total = lax.optimization_barrier(jnp.sum(weights, axis=2))
        accum = jnp.einsum('hrk,khd->hrd', rounded(weights), current[:, 2])
        scores = block_scores(queries, before[:, 0], temper)
        newtop = jnp.maximum(top, lax.optimization_barrier(jnp.max(scores, axis=2)))
        factor = jnp.exp(top - newtop)
        weights = jnp.exp(scores - newtop[:, :, None])
        total = total * factor + lax.optimization_barrier(jnp.sum(weights, axis=2))
        accum = accum * factor[:, :, None] + jnp.einsum('hrk,khd->hrd', rounded(weights), before[:, 1])
        return (accum / total[:, :, None], newtop + jnp.log(total))
    attended, logs = lax.map(per_block, (shaped, earlier))
    attended = jnp.transpose(attended, (0, 2, 1, 3)).reshape(TOKENS, HEADS * HEAD_DIM)
    log_total = jnp.transpose(logs, (1, 0, 2)).reshape(HEADS, TOKENS)
    return (attended, log_total)
```

```python
import functools
import math

import jax
import jax.numpy as jnp
from jax import lax
from jax.experimental import pallas as pl
from jax.experimental.pallas import tpu as pltpu
from jax.sharding import PartitionSpec as P

MESH = pl.DeviceIdType.MESH
HEAD_DIM = 128
N_X, N_Z, N_Y = 4, 6, 8
N_ULY = N_X * N_Z
N_BLK = 32
HALF = N_Z // 2
OWN_SLOT = 1
GROUP = 4
SCALE = math.log2(math.e) / math.sqrt(HEAD_DIM)


def peer(uly, slot, sign):
    x, z = uly // N_Z, lax.rem(uly, N_Z)
    half, place = z // HALF, lax.rem(z, HALF)
    near, turn = lax.rem(slot, 2), slot // 2
    dz, dx = turn // N_X, lax.rem(turn, N_X)
    to_half = jnp.where(near == 1, half, 1 - half)
    to_place = lax.rem(place + sign * dz + HALF, HALF)
    to_x = lax.rem(x + sign * dx + N_X, N_X)
    return to_x * N_Z + to_half * HALF + to_place


def kernel(
    x_ref, o_ref, l_ref, queries, own, prev, stage, top_ref, total_ref,
    loc_sem, q_send, q_recv, kv_send, kv_recv, f_send, f_recv, a_send, a_recv, b_send,
):
    blk, uly = lax.axis_index("blk"), lax.axis_index("uly")
    zhi, y, core = blk // (2 * N_Y), lax.rem(blk // 2, N_Y), lax.rem(blk, 2)
    tokens = x_ref.shape[1]
    following, preceding = lax.rem(blk + 1, N_BLK), lax.rem(blk + N_BLK - 1, N_BLK)
    last = jnp.logical_and(y == N_Y - 1, core == 1)
    first = jnp.logical_and(y == 0, core == 0)
    relay = jnp.logical_and(y != N_Y - 1, core == 1)

    def block_at(zhi_, y_, core_):
        return (zhi_ * N_Y + y_) * 2 + core_

    wrap_source = block_at(zhi, N_Y - 1, 1)
    wrap_target = block_at(1 - zhi, 0, 0)

    barrier = pltpu.get_barrier_semaphore()

    def greet(b, u):
        pl.semaphore_signal(barrier, inc=1, device_id=(b, u), device_id_type=MESH)

    @pl.loop(1, N_ULY)
    def _(k):
        greet(blk, lax.rem(uly + k, N_ULY))

    @pl.when(jnp.logical_not(first))
    def _():
        greet(preceding, uly)

    @pl.when(relay)
    def _():
        greet(wrap_source, uly)

    @pl.when(first)
    def _():
        @pl.loop(0, N_ULY)
        def _(j):
            greet(block_at(1 - zhi, lax.rem(j, N_Y), 1), peer(uly, j, -1))

    pl.semaphore_wait(
        barrier,
        N_ULY - 1 + jnp.where(last, N_Y - 1, 1) + jnp.where(core == 1, N_ULY // N_Y, 0),
    )

    def rows(s):
        return pl.ds(pl.multiple_of(s * tokens, tokens), tokens)

    def head(u):
        return pl.ds(pl.multiple_of(u * HEAD_DIM, HEAD_DIM), HEAD_DIM)

    remote = functools.partial(pltpu.make_async_remote_copy, device_id_type=MESH)

    def send_q(j):
        to = peer(uly, j, 1)
        return remote(
            x_ref.at[0, :, head(to)], queries.at[rows(uly)], q_send.at[j], q_recv.at[j],
            device_id=(blk, to),
        )

    def send_kv(j):
        to = peer(uly, j, 1)
        return remote(
            x_ref.at[1:3, :, head(to)], own.at[:, rows(j)], kv_send.at[j], kv_recv.at[j],
            device_id=(blk, to),
        )

    def forward(j):
        return remote(
            own.at[:, rows(j)], prev.at[:, rows(j)], f_send.at[j], f_recv.at[j],
            device_id=(following, uly),
        )

    def spread(j):
        return remote(
            x_ref.at[1:3, :, head(peer(uly, j, 1))], stage.at[j // N_Y], a_send.at[j],
            a_recv.at[j // N_Y], device_id=(block_at(zhi, lax.rem(j, N_Y), 1), uly),
        )

    def cross_staged(k):
        j = k * N_Y + y
        return remote(
            stage.at[k], prev.at[:, rows(j)], b_send.at[k], f_recv.at[j],
            device_id=(wrap_target, peer(uly, j, 1)),
        )

    def cross_direct(k):
        j = k * N_Y + N_Y - 1
        to = peer(uly, j, 1)
        return remote(
            x_ref.at[1:3, :, head(to)], prev.at[:, rows(j)], b_send.at[k], f_recv.at[j],
            device_id=(wrap_target, to),
        )

    own_q = pltpu.make_async_copy(x_ref.at[0, :, head(uly)], queries.at[rows(uly)], loc_sem.at[0])
    own_kv = pltpu.make_async_copy(
        x_ref.at[1:3, :, head(uly)], own.at[:, rows(OWN_SLOT)], loc_sem.at[1]
    )
    own_q.start()
    own_kv.start()

    @pl.loop(0, N_ULY)
    def _(j):
        @pl.when(j != OWN_SLOT)
        def _():
            send_q(j).start()

        @pl.when(jnp.logical_and(last, lax.rem(j, N_Y) != N_Y - 1))
        def _():
            spread(j).start()

    @pl.when(relay)
    def _():
        @pl.loop(0, N_ULY // N_Y)
        def _(k):
            spread(k * N_Y).wait_recv()
            cross_staged(k).start()

    @pl.when(last)
    def _():
        @pl.loop(0, N_ULY // N_Y)
        def _(k):
            cross_direct(k).start()

    @pl.loop(0, N_ULY)
    def _(j):
        @pl.when(j != OWN_SLOT)
        def _():
            send_kv(j).start()

    own_q.wait()
    own_kv.wait()

    @pl.when(jnp.logical_not(last))
    def _():
        forward(OWN_SLOT).start()

    @pl.loop(0, N_ULY)
    def _(j):
        @pl.when(j != OWN_SLOT)
        def _():
            send_q(j).wait_recv()

    def arrive(g):
        @pl.loop(0, GROUP)
        def _(i):
            j = g * GROUP + i

            @pl.when(j != OWN_SLOT)
            def _():
                send_kv(j).wait_recv()

                @pl.when(jnp.logical_not(last))
                def _():
                    forward(j).start()

    def arrive_prev(g):
        @pl.loop(0, GROUP)
        def _(i):
            forward(g * GROUP + i).wait_recv()

    wide = GROUP * tokens

    def attend(held, g, start):
        span = pl.ds(pl.multiple_of(g * wide, wide), wide)
        scores = lax.dot_general(
            queries[...], held[0, span, :], (((1,), (1,)), ((), ())),
            preferred_element_type=jnp.float32,
        )
        high = jnp.max(scores, axis=1, keepdims=True) * SCALE
        if start:
            new_top = jnp.broadcast_to(high, top_ref.shape)
        else:
            old_top = top_ref[...]
            new_top = jnp.maximum(old_top, high)
            factor = jnp.exp2(old_top - new_top)
        copies = wide // HEAD_DIM
        weights = jnp.exp2(scores * SCALE - jnp.concatenate([new_top] * copies, axis=1))
        part = weights[:, :HEAD_DIM]
        for a in range(1, copies):
            part = part + weights[:, a * HEAD_DIM : (a + 1) * HEAD_DIM]
        product = jnp.dot(
            weights.astype(jnp.bfloat16), held[1, span, :], preferred_element_type=jnp.float32
        )
        top_ref[...] = new_top
        total_ref[...] = part if start else total_ref[...] * factor + part
        o_ref[...] = product if start else o_ref[...] * factor + product

    def step(g, start):
        arrive(g)
        attend(own, g, start)
        arrive_prev(g)
        attend(prev, g, False)

    step(0, True)

    @pl.loop(1, N_ULY // GROUP)
    def _(g):
        step(g, False)

    diagonal = lax.broadcasted_iota(jnp.int32, (HEAD_DIM, HEAD_DIM), 0) == lax.broadcasted_iota(
        jnp.int32, (HEAD_DIM, HEAD_DIM), 1
    )
    for i in range(o_ref.shape[0] // HEAD_DIM):
        span = pl.ds(i * HEAD_DIM, HEAD_DIM)
        total = jnp.sum(total_ref[span, :], axis=1, keepdims=True)
        o_ref[span, :] = o_ref[span, :] / total
        logs = top_ref[span, :] * math.log(2) + jnp.log(total)
        l_ref[:, span] = jnp.sum(jnp.where(diagonal, logs, 0.0), axis=0, keepdims=True)

    @pl.loop(0, N_ULY)
    def _(j):
        @pl.when(j != OWN_SLOT)
        def _():
            send_q(j).wait_send()
            send_kv(j).wait_send()

        @pl.when(jnp.logical_not(last))
        def _():
            forward(j).wait_send()

        @pl.when(jnp.logical_and(last, lax.rem(j, N_Y) != N_Y - 1))
        def _():
            spread(j).wait_send()

    @pl.when(core == 1)
    def _():
        @pl.loop(0, N_ULY // N_Y)
        def _(k):
            cross_staged(k).wait_send()


def shards(qkv):
    tokens, _, width = qkv.shape
    block_len = tokens * N_ULY
    dma = pltpu.SemaphoreType.DMA
    return pl.pallas_call(
        kernel,
        name="regroup_attend",
        out_shape=(
            jax.ShapeDtypeStruct((block_len, HEAD_DIM), jnp.float32),
            jax.ShapeDtypeStruct((1, block_len), jnp.float32),
        ),
        in_specs=[pl.BlockSpec(memory_space=pl.ANY)],
        out_specs=(pl.BlockSpec(memory_space=pltpu.VMEM), pl.BlockSpec(memory_space=pltpu.VMEM)),
        scratch_shapes=[
            pltpu.VMEM((block_len, HEAD_DIM), jnp.bfloat16),
            pltpu.VMEM((2, block_len, HEAD_DIM), jnp.bfloat16),
            pltpu.VMEM((2, block_len, HEAD_DIM), jnp.bfloat16),
            pltpu.VMEM((N_ULY // N_Y, 2, tokens, HEAD_DIM), jnp.bfloat16),
            pltpu.VMEM((block_len, HEAD_DIM), jnp.float32),
            pltpu.VMEM((block_len, HEAD_DIM), jnp.float32),
            dma((2,)),
            dma((N_ULY,)), dma((N_ULY,)), dma((N_ULY,)), dma((N_ULY,)),
            dma((N_ULY,)), dma((N_ULY,)), dma((N_ULY,)),
            dma((N_ULY // N_Y,)), dma((N_ULY // N_Y,)),
        ],
        compiler_params=pltpu.CompilerParams(
            collective_id=0, has_side_effects=True, vmem_limit_bytes=48 << 20
        ),
        cost_estimate=pl.CostEstimate(
            flops=8 * block_len * block_len * HEAD_DIM,
            bytes_accessed=10 * block_len * HEAD_DIM,
            transcendentals=2 * block_len * block_len,
        ),
    )(jnp.transpose(qkv, (1, 0, 2)))


def solution(mesh):
    return jax.shard_map(
        shards,
        mesh=mesh,
        in_specs=(P(("blk", "uly"), None, None),),
        out_specs=(P("blk", "uly"), P("uly", "blk")),
        check_vma=False,
    )
```

```python
import functools
import math

import jax
import jax.numpy as jnp
from jax import lax
from jax.experimental import pallas as pl
from jax.experimental.pallas import tpu as pltpu
from jax.sharding import PartitionSpec as P

MESH = pl.DeviceIdType.MESH
HEAD_DIM = 128
N_X, N_Z, N_Y = 4, 6, 8
N_ULY = N_X * N_Z
N_BLK = 32
HALF = N_Z // 2
OWN_SLOT = 1
GROUP = 4
N_RELAY = 12
EARLY = 8
SCALE = math.log2(math.e) / math.sqrt(HEAD_DIM)


def peer(uly, slot, sign):
    x, z = uly // N_Z, lax.rem(uly, N_Z)
    half, place = z // HALF, lax.rem(z, HALF)
    near, turn = lax.rem(slot, 2), slot // 2
    dz, dx = turn // N_X, lax.rem(turn, N_X)
    to_half = jnp.where(near == 1, half, 1 - half)
    to_place = lax.rem(place + sign * dz + HALF, HALF)
    to_x = lax.rem(x + sign * dx + N_X, N_X)
    return to_x * N_Z + to_half * HALF + to_place


def kernel(
    x_ref, o_ref, l_ref, queries, own, prev, stage, top_ref, total_ref,
    loc_sem, q_send, q_recv, kv_send, kv_recv, f_send, f_recv, a_send, a_recv, b_send, ready,
):
    blk, uly = lax.axis_index("blk"), lax.axis_index("uly")
    zhi, y, core = blk // (2 * N_Y), lax.rem(blk // 2, N_Y), lax.rem(blk, 2)
    tokens = x_ref.shape[1]
    following, preceding = lax.rem(blk + 1, N_BLK), lax.rem(blk + N_BLK - 1, N_BLK)
    last = jnp.logical_and(y == N_Y - 1, core == 1)
    first = jnp.logical_and(y == 0, core == 0)
    relay = jnp.logical_and(y >= 1, y <= N_RELAY // 2)
    relay_slot = 2 * (2 * (y - 1) + core) + 1

    def block_at(zhi_, y_, core_):
        return (zhi_ * N_Y + y_) * 2 + core_

    def relay_at(zhi_, c):
        return block_at(zhi_, 1 + c // 2, lax.rem(c, 2))

    wrap_source = block_at(zhi, N_Y - 1, 1)
    wrap_target = block_at(1 - zhi, 0, 0)
    wrap_origin = block_at(1 - zhi, N_Y - 1, 1)

    barrier = pltpu.get_barrier_semaphore()

    def greet(b, u):
        pl.semaphore_signal(barrier, inc=1, device_id=(b, u), device_id_type=MESH)

    @pl.loop(1, N_ULY)
    def _(k):
        greet(blk, lax.rem(uly + k, N_ULY))

    @pl.when(jnp.logical_not(first))
    def _():
        greet(preceding, uly)

    @pl.when(relay)
    def _():
        greet(wrap_source, uly)
        greet(wrap_target, peer(uly, relay_slot, 1))

    @pl.when(last)
    def _():
        @pl.loop(0, N_RELAY)
        def _(c):
            greet(wrap_target, peer(uly, 2 * c, 1))

    pl.semaphore_wait(
        barrier,
        N_ULY - 1 + jnp.where(last, N_RELAY, 1) + jnp.where(first, N_ULY, 0),
    )

    @pl.when(first)
    def _():
        @pl.loop(0, N_RELAY)
        def _(c):
            pl.semaphore_signal(
                ready, inc=1, device_id=(wrap_origin, peer(uly, 2 * c, -1)), device_id_type=MESH
            )
            pl.semaphore_signal(
                ready, inc=1, device_id=(relay_at(1 - zhi, c), peer(uly, 2 * c + 1, -1)),
                device_id_type=MESH,
            )

    def rows(s):
        return pl.ds(pl.multiple_of(s * tokens, tokens), tokens)

    def head(u):
        return pl.ds(pl.multiple_of(u * HEAD_DIM, HEAD_DIM), HEAD_DIM)

    remote = functools.partial(pltpu.make_async_remote_copy, device_id_type=MESH)

    def send_q(j):
        to = peer(uly, j, 1)
        return remote(
            x_ref.at[0, :, head(to)], queries.at[rows(uly)], q_send.at[j], q_recv.at[j],
            device_id=(blk, to),
        )

    def send_kv(j):
        to = peer(uly, j, 1)
        return remote(
            x_ref.at[1:3, :, head(to)], own.at[:, rows(j)], kv_send.at[j], kv_recv.at[j],
            device_id=(blk, to),
        )

    def forward(j):
        return remote(
            own.at[:, rows(j)], prev.at[:, rows(j)], f_send.at[j], f_recv.at[j],
            device_id=(following, uly),
        )

    def spread(c):
        return remote(
            x_ref.at[1:3, :, head(peer(uly, 2 * c + 1, 1))], stage, a_send.at[c], a_recv,
            device_id=(relay_at(zhi, c), uly),
        )

    def cross_staged():
        return remote(
            stage, prev.at[:, rows(relay_slot)], b_send.at[0], f_recv.at[relay_slot],
            device_id=(wrap_target, peer(uly, relay_slot, 1)),
        )

    def cross_direct(c):
        to = peer(uly, 2 * c, 1)
        return remote(
            x_ref.at[1:3, :, head(to)], prev.at[:, rows(2 * c)], b_send.at[c], f_recv.at[2 * c],
            device_id=(wrap_target, to),
        )

    own_q = pltpu.make_async_copy(x_ref.at[0, :, head(uly)], queries.at[rows(uly)], loc_sem.at[0])
    own_kv = pltpu.make_async_copy(
        x_ref.at[1:3, :, head(uly)], own.at[:, rows(OWN_SLOT)], loc_sem.at[1]
    )
    own_q.start()
    own_kv.start()

    @pl.when(last)
    def _():
        @pl.loop(0, N_RELAY)
        def _(c):
            spread(c).start()

    @pl.loop(0, N_ULY)
    def _(j):
        @pl.when(j != OWN_SLOT)
        def _():
            send_q(j).start()

    @pl.loop(0, EARLY)
    def _(j):
        @pl.when(j != OWN_SLOT)
        def _():
            send_kv(j).start()

    @pl.when(relay)
    def _():
        pl.semaphore_wait(ready, 1)
        spread(0).wait_recv()
        cross_staged().start()

    @pl.when(last)
    def _():
        pl.semaphore_wait(ready, N_RELAY)

    @pl.loop(EARLY, N_ULY)
    def _(j):
        @pl.when(last)
        def _():
            @pl.when(j < EARLY + N_RELAY)
            def _():
                cross_direct(j - EARLY).start()

        send_kv(j).start()

    own_q.wait()
    own_kv.wait()

    @pl.when(jnp.logical_not(last))
    def _():
        forward(OWN_SLOT).start()

    @pl.loop(0, N_ULY)
    def _(j):
        @pl.when(j != OWN_SLOT)
        def _():
            send_q(j).wait_recv()

    def arrive(g):
        @pl.loop(0, GROUP)
        def _(i):
            j = g * GROUP + i

            @pl.when(j != OWN_SLOT)
            def _():
                send_kv(j).wait_recv()

                @pl.when(jnp.logical_not(last))
                def _():
                    forward(j).start()

    def arrive_prev(g):
        @pl.loop(0, GROUP)
        def _(i):
            forward(g * GROUP + i).wait_recv()

    wide = GROUP * tokens

    def attend(held, g, start):
        span = pl.ds(pl.multiple_of(g * wide, wide), wide)
        scores = lax.dot_general(
            queries[...], held[0, span, :], (((1,), (1,)), ((), ())),
            preferred_element_type=jnp.float32,
        )
        high = jnp.max(scores, axis=1, keepdims=True) * SCALE
        if start:
            new_top = jnp.broadcast_to(high, top_ref.shape)
        else:
            old_top = top_ref[...]
            new_top = jnp.maximum(old_top, high)
            factor = jnp.exp2(old_top - new_top)
        copies = wide // HEAD_DIM
        weights = jnp.exp2(scores * SCALE - jnp.concatenate([new_top] * copies, axis=1))
        part = weights[:, :HEAD_DIM]
        for a in range(1, copies):
            part = part + weights[:, a * HEAD_DIM : (a + 1) * HEAD_DIM]
        product = jnp.dot(
            weights.astype(jnp.bfloat16), held[1, span, :], preferred_element_type=jnp.float32
        )
        top_ref[...] = new_top
        total_ref[...] = part if start else total_ref[...] * factor + part
        o_ref[...] = product if start else o_ref[...] * factor + product

    groups = N_ULY // GROUP
    lag = 2
    arrive(0)
    attend(own, 0, True)

    def take_own(g):
        arrive(g)
        attend(own, g, False)

    def take_prev(g):
        arrive_prev(g)
        attend(prev, g, False)

    pl.loop(1, lag)(take_own)

    @pl.loop(lag, groups)
    def _(g):
        take_own(g)
        take_prev(g - lag)

    pl.loop(groups - lag, groups)(take_prev)

    diagonal = lax.broadcasted_iota(jnp.int32, (HEAD_DIM, HEAD_DIM), 0) == lax.broadcasted_iota(
        jnp.int32, (HEAD_DIM, HEAD_DIM), 1
    )
    for i in range(o_ref.shape[0] // HEAD_DIM):
        span = pl.ds(i * HEAD_DIM, HEAD_DIM)
        total = jnp.sum(total_ref[span, :], axis=1, keepdims=True)
        o_ref[span, :] = o_ref[span, :] / total
        logs = top_ref[span, :] * math.log(2) + jnp.log(total)
        l_ref[:, span] = jnp.sum(jnp.where(diagonal, logs, 0.0), axis=0, keepdims=True)

    @pl.loop(0, N_ULY)
    def _(j):
        @pl.when(j != OWN_SLOT)
        def _():
            send_q(j).wait_send()
            send_kv(j).wait_send()

        @pl.when(jnp.logical_not(last))
        def _():
            forward(j).wait_send()

    @pl.when(last)
    def _():
        @pl.loop(0, N_RELAY)
        def _(c):
            spread(c).wait_send()
            cross_direct(c).wait_send()

    @pl.when(relay)
    def _():
        cross_staged().wait_send()


def shards(qkv):
    tokens, _, width = qkv.shape
    block_len = tokens * N_ULY
    dma = pltpu.SemaphoreType.DMA
    return pl.pallas_call(
        kernel,
        name="regroup_attend",
        out_shape=(
            jax.ShapeDtypeStruct((block_len, HEAD_DIM), jnp.float32),
            jax.ShapeDtypeStruct((1, block_len), jnp.float32),
        ),
        in_specs=[pl.BlockSpec(memory_space=pltpu.HBM)],
        out_specs=(pl.BlockSpec(memory_space=pltpu.VMEM), pl.BlockSpec(memory_space=pltpu.VMEM)),
        scratch_shapes=[
            pltpu.VMEM((block_len, HEAD_DIM), jnp.bfloat16),
            pltpu.VMEM((2, block_len, HEAD_DIM), jnp.bfloat16),
            pltpu.VMEM((2, block_len, HEAD_DIM), jnp.bfloat16),
            pltpu.VMEM((2, tokens, HEAD_DIM), jnp.bfloat16),
            pltpu.VMEM((block_len, HEAD_DIM), jnp.float32),
            pltpu.VMEM((block_len, HEAD_DIM), jnp.float32),
            dma((2,)),
            dma((N_ULY,)), dma((N_ULY,)), dma((N_ULY,)), dma((N_ULY,)),
            dma((N_ULY,)), dma((N_ULY,)), dma((N_RELAY,)), dma, dma((N_RELAY,)),
            pltpu.SemaphoreType.REGULAR,
        ],
        compiler_params=pltpu.CompilerParams(
            collective_id=0, has_side_effects=True, vmem_limit_bytes=48 << 20
        ),
        cost_estimate=pl.CostEstimate(
            flops=8 * block_len * block_len * HEAD_DIM,
            bytes_accessed=10 * block_len * HEAD_DIM,
            transcendentals=2 * block_len * block_len,
        ),
    )(jnp.transpose(qkv, (1, 0, 2)))


def solution(mesh):
    return jax.shard_map(
        shards,
        mesh=mesh,
        in_specs=(P(("blk", "uly"), None, None),),
        out_specs=(P("blk", "uly"), P("uly", "blk")),
        check_vma=False,
    )
```

```python
import functools
import math

import jax
import jax.numpy as jnp
from jax import lax
from jax.experimental import pallas as pl
from jax.experimental.pallas import tpu as pltpu
from jax.sharding import PartitionSpec as P

MESH = pl.DeviceIdType.MESH
HEAD_DIM = 128
N_X, N_Z, N_Y = 4, 6, 8
N_ULY = N_X * N_Z
N_BLK = 32
HALF = N_Z // 2
OWN_SLOT = 1
GROUP = 4
N_RELAY = 12
EARLY = 8
SCALE = math.log2(math.e) / math.sqrt(HEAD_DIM)


def peer(uly, slot, sign):
    x, z = uly // N_Z, lax.rem(uly, N_Z)
    half, place = z // HALF, lax.rem(z, HALF)
    near, turn = lax.rem(slot, 2), slot // 2
    dz, dx = turn // N_X, lax.rem(turn, N_X)
    to_half = jnp.where(near == 1, half, 1 - half)
    to_place = lax.rem(place + sign * dz + HALF, HALF)
    to_x = lax.rem(x + sign * dx + N_X, N_X)
    return to_x * N_Z + to_half * HALF + to_place


def kernel(
    x_ref, o_ref, top_ref, total_ref, queries, own, prev, stage,
    loc_sem, q_send, q_recv, kv_send, kv_recv, f_send, f_recv, a_send, a_recv, b_send, ready,
):
    blk, uly = lax.axis_index("blk"), lax.axis_index("uly")
    zhi, y, core = blk // (2 * N_Y), lax.rem(blk // 2, N_Y), lax.rem(blk, 2)
    tokens = x_ref.shape[1]
    following, preceding = lax.rem(blk + 1, N_BLK), lax.rem(blk + N_BLK - 1, N_BLK)
    last = jnp.logical_and(y == N_Y - 1, core == 1)
    first = jnp.logical_and(y == 0, core == 0)
    relay = jnp.logical_and(y >= 1, y <= N_RELAY // 2)
    lower = zhi == 0
    relay_slot = 2 * (2 * (y - 1) + core) + 1

    def block_at(zhi_, y_, core_):
        return (zhi_ * N_Y + y_) * 2 + core_

    def relay_at(zhi_, c):
        return block_at(zhi_, 1 + c // 2, lax.rem(c, 2))

    wrap_source = block_at(zhi, N_Y - 1, 1)
    wrap_target = block_at(1 - zhi, 0, 0)
    wrap_origin = block_at(1 - zhi, N_Y - 1, 1)

    barrier = pltpu.get_barrier_semaphore()

    def greet(b, u):
        pl.semaphore_signal(barrier, inc=1, device_id=(b, u), device_id_type=MESH)

    @pl.loop(1, N_ULY)
    def _(k):
        greet(blk, lax.rem(uly + k, N_ULY))

    @pl.when(jnp.logical_not(first))
    def _():
        greet(preceding, uly)

    @pl.when(relay)
    def _():
        greet(wrap_source, uly)

    @pl.when(jnp.logical_and(relay, lower))
    def _():
        greet(wrap_target, peer(uly, relay_slot, 1))

    @pl.when(jnp.logical_and(last, lower))
    def _():
        @pl.loop(0, N_RELAY)
        def _(c):
            greet(wrap_target, peer(uly, 2 * c, 1))

    @pl.when(jnp.logical_and(first, lower))
    def _():
        @pl.loop(0, N_RELAY)
        def _(c):
            greet(wrap_origin, peer(uly, 2 * c, -1))
            greet(relay_at(1 - zhi, c), peer(uly, 2 * c + 1, -1))

    extra = jnp.where(
        lower, 0, jnp.where(first, N_ULY, jnp.where(last, N_RELAY, jnp.where(relay, 1, 0)))
    )
    pl.semaphore_wait(barrier, N_ULY - 1 + jnp.where(last, N_RELAY, 1) + extra)

    @pl.when(jnp.logical_and(first, jnp.logical_not(lower)))
    def _():
        @pl.loop(0, N_RELAY)
        def _(c):
            pl.semaphore_signal(
                ready, inc=1, device_id=(wrap_origin, peer(uly, 2 * c, -1)), device_id_type=MESH
            )
            pl.semaphore_signal(
                ready, inc=1, device_id=(relay_at(1 - zhi, c), peer(uly, 2 * c + 1, -1)),
                device_id_type=MESH,
            )

    def rows(s):
        return pl.ds(pl.multiple_of(s * tokens, tokens), tokens)

    def head(u):
        return pl.ds(pl.multiple_of(u * HEAD_DIM, HEAD_DIM), HEAD_DIM)

    remote = functools.partial(pltpu.make_async_remote_copy, device_id_type=MESH)

    def send_q(j):
        to = peer(uly, j, 1)
        return remote(
            x_ref.at[0, :, head(to)], queries.at[rows(uly)], q_send.at[j], q_recv.at[j],
            device_id=(blk, to),
        )

    def send_kv(j):
        to = peer(uly, j, 1)
        return remote(
            x_ref.at[1:3, :, head(to)], own.at[:, rows(j)], kv_send.at[j], kv_recv.at[j],
            device_id=(blk, to),
        )

    def forward(j):
        return remote(
            own.at[:, rows(j)], prev.at[:, rows(j)], f_send.at[j], f_recv.at[j],
            device_id=(following, uly),
        )

    def spread(c):
        return remote(
            x_ref.at[1:3, :, head(peer(uly, 2 * c + 1, 1))], stage, a_send.at[c], a_recv,
            device_id=(relay_at(zhi, c), uly),
        )

    def cross_staged():
        return remote(
            stage, prev.at[:, rows(relay_slot)], b_send.at[0], f_recv.at[relay_slot],
            device_id=(wrap_target, peer(uly, relay_slot, 1)),
        )

    def cross_direct(c):
        to = peer(uly, 2 * c, 1)
        return remote(
            x_ref.at[1:3, :, head(to)], prev.at[:, rows(2 * c)], b_send.at[c], f_recv.at[2 * c],
            device_id=(wrap_target, to),
        )

    own_q = pltpu.make_async_copy(x_ref.at[0, :, head(uly)], queries.at[rows(uly)], loc_sem.at[0])
    own_kv = pltpu.make_async_copy(
        x_ref.at[1:3, :, head(uly)], own.at[:, rows(OWN_SLOT)], loc_sem.at[1]
    )
    own_q.start()
    own_kv.start()

    @pl.when(last)
    def _():
        @pl.loop(0, N_RELAY)
        def _(c):
            spread(c).start()

    @pl.loop(0, N_ULY)
    def _(j):
        @pl.when(j != OWN_SLOT)
        def _():
            send_q(j).start()

    @pl.loop(0, EARLY)
    def _(j):
        @pl.when(j != OWN_SLOT)
        def _():
            send_kv(j).start()

    @pl.when(relay)
    def _():
        @pl.when(lower)
        def _():
            pl.semaphore_wait(ready, 1)

        spread(0).wait_recv()
        cross_staged().start()

    @pl.when(jnp.logical_and(last, lower))
    def _():
        pl.semaphore_wait(ready, N_RELAY)

    @pl.loop(EARLY, N_ULY)
    def _(j):
        @pl.when(last)
        def _():
            @pl.when(j < EARLY + N_RELAY)
            def _():
                cross_direct(j - EARLY).start()

        send_kv(j).start()

    own_q.wait()
    own_kv.wait()

    @pl.when(jnp.logical_not(last))
    def _():
        forward(OWN_SLOT).start()

    @pl.loop(0, N_ULY)
    def _(j):
        @pl.when(j != OWN_SLOT)
        def _():
            send_q(j).wait_recv()

    def arrive(g):
        @pl.loop(0, GROUP)
        def _(i):
            j = g * GROUP + i

            @pl.when(j != OWN_SLOT)
            def _():
                send_kv(j).wait_recv()

                @pl.when(jnp.logical_not(last))
                def _():
                    forward(j).start()

    def arrive_prev(g):
        @pl.loop(0, GROUP)
        def _(i):
            forward(g * GROUP + i).wait_recv()

    wide = GROUP * tokens

    def attend(held, g, start):
        span = pl.ds(pl.multiple_of(g * wide, wide), wide)
        scores = lax.dot_general(
            queries[...], held[0, span, :], (((1,), (1,)), ((), ())),
            preferred_element_type=jnp.float32,
        )
        high = jnp.max(scores, axis=1, keepdims=True) * SCALE
        if start:
            new_top = jnp.broadcast_to(high, top_ref.shape)
        else:
            old_top = top_ref[...]
            new_top = jnp.maximum(old_top, high)
            factor = jnp.exp2(old_top - new_top)
        copies = wide // HEAD_DIM
        weights = jnp.exp2(scores * SCALE - jnp.concatenate([new_top] * copies, axis=1))
        part = weights[:, :HEAD_DIM]
        for a in range(1, copies):
            part = part + weights[:, a * HEAD_DIM : (a + 1) * HEAD_DIM]
        product = jnp.dot(
            weights.astype(jnp.bfloat16), held[1, span, :], preferred_element_type=jnp.float32
        )
        top_ref[...] = new_top
        total_ref[...] = part if start else total_ref[...] * factor + part
        o_ref[...] = product if start else o_ref[...] * factor + product

    groups = N_ULY // GROUP
    lag = 3
    arrive(0)
    attend(own, 0, True)

    def take_own(g):
        arrive(g)
        attend(own, g, False)

    def take_prev(g):
        arrive_prev(g)
        attend(prev, g, False)

    pl.loop(1, lag)(take_own)

    @pl.loop(lag, groups - 1)
    def _(g):
        take_own(g)
        take_prev(g - lag)

    take_prev(groups - 1 - lag)
    take_own(groups - 1)
    pl.loop(groups - lag, groups)(take_prev)

    @pl.loop(0, N_ULY)
    def _(j):
        @pl.when(j != OWN_SLOT)
        def _():
            send_q(j).wait_send()
            send_kv(j).wait_send()

        @pl.when(jnp.logical_not(last))
        def _():
            forward(j).wait_send()

    @pl.when(last)
    def _():
        @pl.loop(0, N_RELAY)
        def _(c):
            spread(c).wait_send()
            cross_direct(c).wait_send()

    @pl.when(relay)
    def _():
        cross_staged().wait_send()


def finish(a_ref, top_ref, total_ref, o_ref, l_ref):
    diagonal = lax.broadcasted_iota(jnp.int32, (HEAD_DIM, HEAD_DIM), 0) == lax.broadcasted_iota(
        jnp.int32, (HEAD_DIM, HEAD_DIM), 1
    )
    for i in range(o_ref.shape[0] // HEAD_DIM):
        span = pl.ds(i * HEAD_DIM, HEAD_DIM)
        total = jnp.sum(total_ref[span, :], axis=1, keepdims=True)
        o_ref[span, :] = a_ref[span, :] / total
        logs = top_ref[span, :] * math.log(2) + jnp.log(total)
        l_ref[:, span] = jnp.sum(jnp.where(diagonal, logs, 0.0), axis=0, keepdims=True)


def shards(qkv):
    tokens, _, width = qkv.shape
    block_len = tokens * N_ULY
    dma = pltpu.SemaphoreType.DMA
    in_vmem = pl.BlockSpec(memory_space=pltpu.VMEM)
    rows = jax.ShapeDtypeStruct((block_len, HEAD_DIM), jnp.float32)
    parts = pl.pallas_call(
        kernel,
        name="regroup_attend",
        out_shape=(rows, rows, rows),
        in_specs=[pl.BlockSpec(memory_space=pltpu.HBM)],
        out_specs=(in_vmem, in_vmem, in_vmem),
        scratch_shapes=[
            pltpu.VMEM((block_len, HEAD_DIM), jnp.bfloat16),
            pltpu.VMEM((2, block_len, HEAD_DIM), jnp.bfloat16),
            pltpu.VMEM((2, block_len, HEAD_DIM), jnp.bfloat16),
            pltpu.VMEM((2, tokens, HEAD_DIM), jnp.bfloat16),
            dma((2,)),
            dma((N_ULY,)), dma((N_ULY,)), dma((N_ULY,)), dma((N_ULY,)),
            dma((N_ULY,)), dma((N_ULY,)), dma((N_RELAY,)), dma, dma((N_RELAY,)),
            pltpu.SemaphoreType.REGULAR,
        ],
        compiler_params=pltpu.CompilerParams(
            collective_id=0, has_side_effects=True, vmem_limit_bytes=48 << 20
        ),
        cost_estimate=pl.CostEstimate(
            flops=8 * block_len * block_len * HEAD_DIM,
            bytes_accessed=10 * block_len * HEAD_DIM,
            transcendentals=2 * block_len * block_len,
        ),
    )(pltpu.with_memory_space_constraint(jnp.transpose(qkv, (1, 0, 2)), pltpu.HBM))
    return pl.pallas_call(
        finish,
        name="finish",
        out_shape=(rows, jax.ShapeDtypeStruct((1, block_len), jnp.float32)),
        in_specs=[in_vmem] * 3,
        out_specs=(in_vmem, in_vmem),
        compiler_params=pltpu.CompilerParams(vmem_limit_bytes=8 << 20),
    )(*parts)


def solution(mesh):
    return jax.shard_map(
        shards,
        mesh=mesh,
        in_specs=(P(("blk", "uly"), None, None),),
        out_specs=(P("blk", "uly"), P("uly", "blk")),
        check_vma=False,
    )
```

```python
import functools
import math

import jax
import jax.numpy as jnp
from jax import lax
from jax.experimental import pallas as pl
from jax.experimental.pallas import tpu as pltpu
from jax.sharding import PartitionSpec as P

MESH = pl.DeviceIdType.MESH
HEAD_DIM = 128
N_X, N_Z, N_Y = 4, 6, 8
N_ULY = N_X * N_Z
N_BLK = 32
HALF = N_Z // 2
OWN_SLOT = 0
GROUP = 4
N_RELAY = 12
EARLY = 4
SCALE = math.log2(math.e) / math.sqrt(HEAD_DIM)


def peer(uly, slot, sign):
    x, z = uly // N_Z, lax.rem(uly, N_Z)
    half, place = z // HALF, lax.rem(z, HALF)
    near, turn = 1 - slot // 12, lax.rem(slot, 12)
    dz, dx = turn // N_X, lax.rem(turn, N_X)
    to_half = jnp.where(near == 1, half, 1 - half)
    to_place = lax.rem(place + sign * dz + HALF, HALF)
    to_x = lax.rem(x + sign * dx + N_X, N_X)
    return to_x * N_Z + to_half * HALF + to_place


def kernel(
    x_ref, o_ref, top_ref, total_ref, queries, own, prev, stage,
    loc_sem, q_send, q_recv, kv_send, kv_recv, f_send, f_recv, a_send, a_recv, b_send, ready,
):
    blk, uly = lax.axis_index("blk"), lax.axis_index("uly")
    zhi, y, core = blk // (2 * N_Y), lax.rem(blk // 2, N_Y), lax.rem(blk, 2)
    tokens = x_ref.shape[1]
    following, preceding = lax.rem(blk + 1, N_BLK), lax.rem(blk + N_BLK - 1, N_BLK)
    last = jnp.logical_and(y == N_Y - 1, core == 1)
    first = jnp.logical_and(y == 0, core == 0)
    relay = jnp.logical_and(y >= 1, y <= N_RELAY // 2)
    lower = zhi == 0
    relay_slot = 2 * (y - 1) + core + 0

    def block_at(zhi_, y_, core_):
        return (zhi_ * N_Y + y_) * 2 + core_

    def relay_at(zhi_, c):
        return block_at(zhi_, 1 + c // 2, lax.rem(c, 2))

    wrap_source = block_at(zhi, N_Y - 1, 1)
    wrap_target = block_at(1 - zhi, 0, 0)
    wrap_origin = block_at(1 - zhi, N_Y - 1, 1)

    barrier = pltpu.get_barrier_semaphore()

    def greet(b, u):
        pl.semaphore_signal(barrier, inc=1, device_id=(b, u), device_id_type=MESH)

    @pl.loop(1, N_ULY)
    def _(k):
        greet(blk, lax.rem(uly + k, N_ULY))

    @pl.when(jnp.logical_not(first))
    def _():
        greet(preceding, uly)

    @pl.when(relay)
    def _():
        greet(wrap_source, uly)

    @pl.when(jnp.logical_and(relay, lower))
    def _():
        greet(wrap_target, peer(uly, relay_slot, 1))

    @pl.when(jnp.logical_and(last, lower))
    def _():
        @pl.loop(0, N_RELAY)
        def _(c):
            greet(wrap_target, peer(uly, c + 12, 1))

    @pl.when(jnp.logical_and(first, lower))
    def _():
        @pl.loop(0, N_RELAY)
        def _(c):
            greet(wrap_origin, peer(uly, c + 12, -1))
            greet(relay_at(1 - zhi, c), peer(uly, (c + 0), -1))

    extra = jnp.where(
        lower, 0, jnp.where(first, N_ULY, jnp.where(last, N_RELAY, jnp.where(relay, 1, 0)))
    )
    pl.semaphore_wait(barrier, N_ULY - 1 + jnp.where(last, N_RELAY, 1) + extra)

    @pl.when(jnp.logical_and(first, jnp.logical_not(lower)))
    def _():
        @pl.loop(0, N_RELAY)
        def _(c):
            pl.semaphore_signal(
                ready, inc=1, device_id=(wrap_origin, peer(uly, c + 12, -1)), device_id_type=MESH
            )
            pl.semaphore_signal(
                ready, inc=1, device_id=(relay_at(1 - zhi, c), peer(uly, (c + 0), -1)),
                device_id_type=MESH,
            )

    def rows(s):
        return pl.ds(pl.multiple_of(s * tokens, tokens), tokens)

    def head(u):
        return pl.ds(pl.multiple_of(u * HEAD_DIM, HEAD_DIM), HEAD_DIM)

    remote = functools.partial(pltpu.make_async_remote_copy, device_id_type=MESH)

    def send_q(j):
        to = peer(uly, j, 1)
        return remote(
            x_ref.at[0, :, head(to)], queries.at[rows(uly)], q_send.at[j], q_recv.at[j],
            device_id=(blk, to),
        )

    def send_kv(j):
        to = peer(uly, j, 1)
        return remote(
            x_ref.at[1:3, :, head(to)], own.at[:, rows(j)], kv_send.at[j], kv_recv.at[j],
            device_id=(blk, to),
        )

    def forward(j):
        return remote(
            own.at[:, rows(j)], prev.at[:, rows(j)], f_send.at[j], f_recv.at[j],
            device_id=(following, uly),
        )

    def spread(c):
        return remote(
            x_ref.at[1:3, :, head(peer(uly, (c + 0), 1))], stage, a_send.at[c], a_recv,
            device_id=(relay_at(zhi, c), uly),
        )

    def cross_staged():
        return remote(
            stage, prev.at[:, rows(relay_slot)], b_send.at[0], f_recv.at[relay_slot],
            device_id=(wrap_target, peer(uly, relay_slot, 1)),
        )

    def cross_direct(c):
        to = peer(uly, c + 12, 1)
        return remote(
            x_ref.at[1:3, :, head(to)], prev.at[:, rows((c + 12))], b_send.at[c], f_recv.at[c + 12],
            device_id=(wrap_target, to),
        )

    own_q = pltpu.make_async_copy(x_ref.at[0, :, head(uly)], queries.at[rows(uly)], loc_sem.at[0])
    own_kv = pltpu.make_async_copy(
        x_ref.at[1:3, :, head(uly)], own.at[:, rows(OWN_SLOT)], loc_sem.at[1]
    )
    own_q.start()
    own_kv.start()

    @pl.when(last)
    def _():
        @pl.loop(0, N_RELAY)
        def _(c):
            spread(c).start()

    @pl.when(jnp.logical_and(last, jnp.logical_not(lower)))
    def _():
        @pl.loop(0, N_RELAY)
        def _(c):
            cross_direct(c).start()

    @pl.loop(0, N_ULY)
    def _(i):
        j = lax.rem(i + N_ULY // 2, N_ULY)

        @pl.when(j != OWN_SLOT)
        def _():
            send_q(j).start()

    @pl.loop(0, EARLY)
    def _(j):
        @pl.when(j != OWN_SLOT)
        def _():
            send_kv(j).start()

    @pl.when(relay)
    def _():
        @pl.when(lower)
        def _():
            pl.semaphore_wait(ready, 1)

        spread(0).wait_recv()
        cross_staged().start()

    @pl.when(jnp.logical_and(last, lower))
    def _():
        pl.semaphore_wait(ready, N_RELAY)

    @pl.loop(EARLY, N_ULY)
    def _(j):
        @pl.when(jnp.logical_and(last, lower))
        def _():
            @pl.when(j < EARLY + N_RELAY)
            def _():
                cross_direct(j - EARLY).start()

        @pl.when(j != OWN_SLOT)
        def _():
            send_kv(j).start()

    own_q.wait()
    own_kv.wait()

    @pl.when(jnp.logical_not(last))
    def _():
        forward(OWN_SLOT).start()

    @pl.loop(0, N_ULY)
    def _(j):
        @pl.when(j != OWN_SLOT)
        def _():
            send_q(j).wait_recv()

    def arrive(g):
        @pl.loop(0, GROUP)
        def _(i):
            j = g * GROUP + i

            @pl.when(j != OWN_SLOT)
            def _():
                send_kv(j).wait_recv()

                @pl.when(jnp.logical_not(last))
                def _():
                    forward(j).start()

    def arrive_prev(g):
        @pl.loop(0, GROUP)
        def _(i):
            forward(g * GROUP + i).wait_recv()

    wide = GROUP * tokens

    def attend(held, g, start):
        span = pl.ds(pl.multiple_of(g * wide, wide), wide)
        scores = lax.dot_general(
            queries[...], held[0, span, :], (((1,), (1,)), ((), ())),
            preferred_element_type=jnp.float32,
        )
        high = jnp.max(scores, axis=1, keepdims=True) * SCALE
        if start:
            new_top = jnp.broadcast_to(high, top_ref.shape)
        else:
            old_top = top_ref[...]
            new_top = jnp.maximum(old_top, high)
            factor = jnp.exp2(old_top - new_top)
        copies = wide // HEAD_DIM
        weights = jnp.exp2(scores * SCALE - jnp.concatenate([new_top] * copies, axis=1))
        part = weights[:, :HEAD_DIM]
        for a in range(1, copies):
            part = part + weights[:, a * HEAD_DIM : (a + 1) * HEAD_DIM]
        product = jnp.dot(
            weights.astype(jnp.bfloat16), held[1, span, :], preferred_element_type=jnp.float32
        )
        top_ref[...] = new_top
        total_ref[...] = part if start else total_ref[...] * factor + part
        o_ref[...] = product if start else o_ref[...] * factor + product

    groups = N_ULY // GROUP
    lag = 2
    arrive(0)
    attend(own, 0, True)

    def take_own(g):
        arrive(g)
        attend(own, g, False)

    def take_prev(g):
        arrive_prev(g)
        attend(prev, g, False)

    pl.loop(1, lag)(take_own)

    @pl.loop(lag, groups - 1)
    def _(g):
        take_own(g)
        take_prev(g - lag)

    take_prev(groups - 1 - lag)
    take_own(groups - 1)
    pl.loop(groups - lag, groups)(take_prev)

    @pl.loop(0, N_ULY)
    def _(j):
        @pl.when(j != OWN_SLOT)
        def _():
            send_q(j).wait_send()
            send_kv(j).wait_send()

        @pl.when(jnp.logical_not(last))
        def _():
            forward(j).wait_send()

    @pl.when(last)
    def _():
        @pl.loop(0, N_RELAY)
        def _(c):
            spread(c).wait_send()
            cross_direct(c).wait_send()

    @pl.when(relay)
    def _():
        cross_staged().wait_send()


def finish(a_ref, top_ref, total_ref, o_ref, l_ref):
    diagonal = lax.broadcasted_iota(jnp.int32, (HEAD_DIM, HEAD_DIM), 0) == lax.broadcasted_iota(
        jnp.int32, (HEAD_DIM, HEAD_DIM), 1
    )
    for i in range(o_ref.shape[0] // HEAD_DIM):
        span = pl.ds(i * HEAD_DIM, HEAD_DIM)
        total = jnp.sum(total_ref[span, :], axis=1, keepdims=True)
        o_ref[span, :] = a_ref[span, :] / total
        logs = top_ref[span, :] * math.log(2) + jnp.log(total)
        l_ref[:, span] = jnp.sum(jnp.where(diagonal, logs, 0.0), axis=0, keepdims=True)


def shards(qkv):
    tokens, _, width = qkv.shape
    block_len = tokens * N_ULY
    dma = pltpu.SemaphoreType.DMA
    in_vmem = pl.BlockSpec(memory_space=pltpu.VMEM)
    rows = jax.ShapeDtypeStruct((block_len, HEAD_DIM), jnp.float32)
    parts = pl.pallas_call(
        kernel,
        name="regroup_attend",
        out_shape=(rows, rows, rows),
        in_specs=[pl.BlockSpec(memory_space=pltpu.HBM)],
        out_specs=(in_vmem, in_vmem, in_vmem),
        scratch_shapes=[
            pltpu.VMEM((block_len, HEAD_DIM), jnp.bfloat16),
            pltpu.VMEM((2, block_len, HEAD_DIM), jnp.bfloat16),
            pltpu.VMEM((2, block_len, HEAD_DIM), jnp.bfloat16),
            pltpu.VMEM((2, tokens, HEAD_DIM), jnp.bfloat16),
            dma((2,)),
            dma((N_ULY,)), dma((N_ULY,)), dma((N_ULY,)), dma((N_ULY,)),
            dma((N_ULY,)), dma((N_ULY,)), dma((N_RELAY,)), dma, dma((N_RELAY,)),
            pltpu.SemaphoreType.REGULAR,
        ],
        compiler_params=pltpu.CompilerParams(
            collective_id=0, has_side_effects=True, vmem_limit_bytes=48 << 20
        ),
        cost_estimate=pl.CostEstimate(
            flops=8 * block_len * block_len * HEAD_DIM,
            bytes_accessed=10 * block_len * HEAD_DIM,
            transcendentals=2 * block_len * block_len,
        ),
    )(pltpu.with_memory_space_constraint(jnp.transpose(qkv, (1, 0, 2)), pltpu.HBM))
    return pl.pallas_call(
        finish,
        name="finish",
        out_shape=(rows, jax.ShapeDtypeStruct((1, block_len), jnp.float32)),
        in_specs=[in_vmem] * 3,
        out_specs=(in_vmem, in_vmem),
        compiler_params=pltpu.CompilerParams(vmem_limit_bytes=8 << 20),
    )(*parts)


def solution(mesh):
    return jax.shard_map(
        shards,
        mesh=mesh,
        in_specs=(P(("blk", "uly"), None, None),),
        out_specs=(P("blk", "uly"), P("uly", "blk")),
        check_vma=False,
    )
```

```python
import functools
import math

import jax
import jax.numpy as jnp
from jax import lax
from jax.experimental import pallas as pl
from jax.experimental.pallas import tpu as pltpu
from jax.sharding import PartitionSpec as P

MESH = pl.DeviceIdType.MESH
HEAD_DIM = 128
N_X, N_Z, N_Y = 4, 6, 8
N_ULY = N_X * N_Z
N_BLK = 32
HALF = N_Z // 2
OWN_SLOT = 0
GROUP = 4
N_RELAY = 12
EARLY = 12
SCALE = math.log2(math.e) / math.sqrt(HEAD_DIM)


def peer(uly, slot, sign):
    x, z = uly // N_Z, lax.rem(uly, N_Z)
    half, place = z // HALF, lax.rem(z, HALF)
    near, turn = 1 - slot // 12, lax.rem(slot, 12)
    dz, dx = turn // N_X, lax.rem(turn, N_X)
    to_half = jnp.where(near == 1, half, 1 - half)
    to_place = lax.rem(place + sign * dz + HALF, HALF)
    to_x = lax.rem(x + sign * dx + N_X, N_X)
    return to_x * N_Z + to_half * HALF + to_place


def kernel(
    x_ref, o_ref, top_ref, total_ref, queries, own, prev, stage,
    loc_sem, q_send, q_recv, kv_send, kv_recv, f_send, f_recv, a_send, a_recv, b_send, ready,
):
    blk, uly = lax.axis_index("blk"), lax.axis_index("uly")
    zhi, y, core = blk // (2 * N_Y), lax.rem(blk // 2, N_Y), lax.rem(blk, 2)
    tokens = x_ref.shape[1]
    following, preceding = lax.rem(blk + 1, N_BLK), lax.rem(blk + N_BLK - 1, N_BLK)
    last = jnp.logical_and(y == N_Y - 1, core == 1)
    first = jnp.logical_and(y == 0, core == 0)
    relay = jnp.logical_and(y >= 1, y <= N_RELAY // 2)
    lower = zhi == 0
    relay_slot = 2 * (y - 1) + core + 0

    def block_at(zhi_, y_, core_):
        return (zhi_ * N_Y + y_) * 2 + core_

    def relay_at(zhi_, c):
        return block_at(zhi_, 1 + c // 2, lax.rem(c, 2))

    wrap_source = block_at(zhi, N_Y - 1, 1)
    wrap_target = block_at(1 - zhi, 0, 0)
    wrap_origin = block_at(1 - zhi, N_Y - 1, 1)

    barrier = pltpu.get_barrier_semaphore()

    def greet(b, u):
        pl.semaphore_signal(barrier, inc=1, device_id=(b, u), device_id_type=MESH)

    @pl.loop(1, N_ULY)
    def _(k):
        greet(blk, lax.rem(uly + k, N_ULY))

    @pl.when(jnp.logical_not(first))
    def _():
        greet(preceding, uly)

    @pl.when(relay)
    def _():
        greet(wrap_source, uly)

    @pl.when(jnp.logical_and(relay, lower))
    def _():
        greet(wrap_target, peer(uly, relay_slot, 1))

    @pl.when(jnp.logical_and(last, lower))
    def _():
        @pl.loop(0, N_RELAY)
        def _(c):
            greet(wrap_target, peer(uly, c + 12, 1))

    @pl.when(jnp.logical_and(first, lower))
    def _():
        @pl.loop(0, N_RELAY)
        def _(c):
            greet(wrap_origin, peer(uly, c + 12, -1))
            greet(relay_at(1 - zhi, c), peer(uly, (c + 0), -1))

    extra = jnp.where(
        lower, 0, jnp.where(first, N_ULY, jnp.where(last, N_RELAY, jnp.where(relay, 1, 0)))
    )
    pl.semaphore_wait(barrier, N_ULY - 1 + jnp.where(last, N_RELAY, 1) + extra)

    @pl.when(jnp.logical_and(first, jnp.logical_not(lower)))
    def _():
        @pl.loop(0, N_RELAY)
        def _(c):
            pl.semaphore_signal(
                ready, inc=1, device_id=(wrap_origin, peer(uly, c + 12, -1)), device_id_type=MESH
            )
            pl.semaphore_signal(
                ready, inc=1, device_id=(relay_at(1 - zhi, c), peer(uly, (c + 0), -1)),
                device_id_type=MESH,
            )

    def rows(s):
        return pl.ds(pl.multiple_of(s * tokens, tokens), tokens)

    def head(u):
        return pl.ds(pl.multiple_of(u * HEAD_DIM, HEAD_DIM), HEAD_DIM)

    remote = functools.partial(pltpu.make_async_remote_copy, device_id_type=MESH)

    def send_q(j):
        to = peer(uly, j, 1)
        return remote(
            x_ref.at[0, :, head(to)], queries.at[rows(uly)], q_send.at[j], q_recv.at[j],
            device_id=(blk, to),
        )

    def send_kv(j):
        to = peer(uly, j, 1)
        return remote(
            x_ref.at[1:3, :, head(to)], own.at[:, rows(j)], kv_send.at[j], kv_recv.at[j],
            device_id=(blk, to),
        )

    def forward(j):
        return remote(
            own.at[:, rows(j)], prev.at[:, rows(j)], f_send.at[j], f_recv.at[j],
            device_id=(following, uly),
        )

    def spread(c):
        return remote(
            x_ref.at[1:3, :, head(peer(uly, (c + 0), 1))], stage, a_send.at[c], a_recv,
            device_id=(relay_at(zhi, c), uly),
        )

    def cross_staged():
        return remote(
            stage, prev.at[:, rows(relay_slot)], b_send.at[0], f_recv.at[relay_slot],
            device_id=(wrap_target, peer(uly, relay_slot, 1)),
        )

    def cross_direct(c):
        to = peer(uly, c + 12, 1)
        return remote(
            x_ref.at[1:3, :, head(to)], prev.at[:, rows((c + 12))], b_send.at[c], f_recv.at[c + 12],
            device_id=(wrap_target, to),
        )

    own_q = pltpu.make_async_copy(x_ref.at[0, :, head(uly)], queries.at[rows(uly)], loc_sem.at[0])
    own_kv = pltpu.make_async_copy(
        x_ref.at[1:3, :, head(uly)], own.at[:, rows(OWN_SLOT)], loc_sem.at[1]
    )
    own_q.start()
    own_kv.start()

    @pl.when(last)
    def _():
        @pl.loop(0, N_RELAY)
        def _(c):
            spread(c).start()

    @pl.when(jnp.logical_and(last, jnp.logical_not(lower)))
    def _():
        @pl.loop(0, N_RELAY)
        def _(c):
            cross_direct(c).start()

    @pl.loop(0, N_ULY)
    def _(i):
        j = lax.rem(i + N_ULY // 2, N_ULY)

        @pl.when(j != OWN_SLOT)
        def _():
            send_q(j).start()

    @pl.loop(0, EARLY)
    def _(j):
        @pl.when(j != OWN_SLOT)
        def _():
            send_kv(j).start()

    @pl.when(relay)
    def _():
        @pl.when(lower)
        def _():
            pl.semaphore_wait(ready, 1)

        spread(0).wait_recv()
        cross_staged().start()

    @pl.when(jnp.logical_and(last, lower))
    def _():
        pl.semaphore_wait(ready, N_RELAY)

    @pl.loop(EARLY, N_ULY)
    def _(j):
        @pl.when(jnp.logical_and(last, lower))
        def _():
            @pl.when(j < EARLY + N_RELAY)
            def _():
                cross_direct(j - EARLY).start()

        @pl.when(j != OWN_SLOT)
        def _():
            send_kv(j).start()

    own_q.wait()
    own_kv.wait()

    @pl.when(jnp.logical_not(last))
    def _():
        forward(OWN_SLOT).start()

    @pl.loop(0, N_ULY)
    def _(j):
        @pl.when(j != OWN_SLOT)
        def _():
            send_q(j).wait_recv()

    def arrive(g):
        @pl.loop(0, GROUP)
        def _(i):
            j = g * GROUP + i

            @pl.when(j != OWN_SLOT)
            def _():
                send_kv(j).wait_recv()

                @pl.when(jnp.logical_not(last))
                def _():
                    forward(j).start()

    def arrive_prev(g):
        @pl.loop(0, GROUP)
        def _(i):
            forward(g * GROUP + i).wait_recv()

    wide = GROUP * tokens

    def attend(held, g, start):
        span = pl.ds(pl.multiple_of(g * wide, wide), wide)
        scores = lax.dot_general(
            queries[...], held[0, span, :], (((1,), (1,)), ((), ())),
            preferred_element_type=jnp.float32,
        )
        high = jnp.max(scores, axis=1, keepdims=True) * SCALE
        if start:
            new_top = jnp.broadcast_to(high, top_ref.shape)
        else:
            old_top = top_ref[...]
            new_top = jnp.maximum(old_top, high)
            factor = jnp.exp2(old_top - new_top)
        copies = wide // HEAD_DIM
        weights = jnp.exp2(scores * SCALE - jnp.concatenate([new_top] * copies, axis=1))
        part = weights[:, :HEAD_DIM]
        for a in range(1, copies):
            part = part + weights[:, a * HEAD_DIM : (a + 1) * HEAD_DIM]
        product = jnp.dot(
            weights.astype(jnp.bfloat16), held[1, span, :], preferred_element_type=jnp.float32
        )
        top_ref[...] = new_top
        total_ref[...] = part if start else total_ref[...] * factor + part
        o_ref[...] = product if start else o_ref[...] * factor + product

    groups = N_ULY // GROUP
    lag = 2
    arrive(0)
    attend(own, 0, True)

    def take_own(g):
        arrive(g)
        attend(own, g, False)

    def take_prev(g):
        arrive_prev(g)
        attend(prev, g, False)

    pl.loop(1, lag)(take_own)

    @pl.loop(lag, groups - 1)
    def _(g):
        take_own(g)
        take_prev(g - lag)

    take_prev(groups - 1 - lag)
    take_own(groups - 1)
    pl.loop(groups - lag, groups)(take_prev)

    @pl.loop(0, N_ULY)
    def _(j):
        @pl.when(j != OWN_SLOT)
        def _():
            send_q(j).wait_send()
            send_kv(j).wait_send()

        @pl.when(jnp.logical_not(last))
        def _():
            forward(j).wait_send()

    @pl.when(last)
    def _():
        @pl.loop(0, N_RELAY)
        def _(c):
            spread(c).wait_send()
            cross_direct(c).wait_send()

    @pl.when(relay)
    def _():
        cross_staged().wait_send()


def finish(a_ref, top_ref, total_ref, o_ref, l_ref):
    diagonal = lax.broadcasted_iota(jnp.int32, (HEAD_DIM, HEAD_DIM), 0) == lax.broadcasted_iota(
        jnp.int32, (HEAD_DIM, HEAD_DIM), 1
    )
    for i in range(o_ref.shape[0] // HEAD_DIM):
        span = pl.ds(i * HEAD_DIM, HEAD_DIM)
        total = jnp.sum(total_ref[span, :], axis=1, keepdims=True)
        o_ref[span, :] = a_ref[span, :] / total
        logs = top_ref[span, :] * math.log(2) + jnp.log(total)
        l_ref[:, span] = jnp.sum(jnp.where(diagonal, logs, 0.0), axis=0, keepdims=True)


def shards(qkv):
    tokens, _, width = qkv.shape
    block_len = tokens * N_ULY
    dma = pltpu.SemaphoreType.DMA
    in_vmem = pl.BlockSpec(memory_space=pltpu.VMEM)
    rows = jax.ShapeDtypeStruct((block_len, HEAD_DIM), jnp.float32)
    parts = pl.pallas_call(
        kernel,
        name="regroup_attend",
        out_shape=(rows, rows, rows),
        in_specs=[pl.BlockSpec(memory_space=pltpu.HBM)],
        out_specs=(in_vmem, in_vmem, in_vmem),
        scratch_shapes=[
            pltpu.VMEM((block_len, HEAD_DIM), jnp.bfloat16),
            pltpu.VMEM((2, block_len, HEAD_DIM), jnp.bfloat16),
            pltpu.VMEM((2, block_len, HEAD_DIM), jnp.bfloat16),
            pltpu.VMEM((2, tokens, HEAD_DIM), jnp.bfloat16),
            dma((2,)),
            dma((N_ULY,)), dma((N_ULY,)), dma((N_ULY,)), dma((N_ULY,)),
            dma((N_ULY,)), dma((N_ULY,)), dma((N_RELAY,)), dma, dma((N_RELAY,)),
            pltpu.SemaphoreType.REGULAR,
        ],
        compiler_params=pltpu.CompilerParams(
            collective_id=0, has_side_effects=True, vmem_limit_bytes=48 << 20
        ),
        cost_estimate=pl.CostEstimate(
            flops=8 * block_len * block_len * HEAD_DIM,
            bytes_accessed=10 * block_len * HEAD_DIM,
            transcendentals=2 * block_len * block_len,
        ),
    )(pltpu.with_memory_space_constraint(jnp.transpose(qkv, (1, 0, 2)), pltpu.HBM))
    return pl.pallas_call(
        finish,
        name="finish",
        out_shape=(rows, jax.ShapeDtypeStruct((1, block_len), jnp.float32)),
        in_specs=[in_vmem] * 3,
        out_specs=(in_vmem, in_vmem),
        compiler_params=pltpu.CompilerParams(vmem_limit_bytes=8 << 20),
    )(*parts)


def solution(mesh):
    return jax.shard_map(
        shards,
        mesh=mesh,
        in_specs=(P(("blk", "uly"), None, None),),
        out_specs=(P("blk", "uly"), P("uly", "blk")),
        check_vma=False,
    )
```

```python
import functools
import math

import jax
import jax.numpy as jnp
from jax import lax
from jax.experimental import pallas as pl
from jax.experimental.pallas import tpu as pltpu
from jax.sharding import PartitionSpec as P

MESH = pl.DeviceIdType.MESH
HEAD_DIM = 128
N_X, N_Z, N_Y = 4, 6, 8
N_ULY = N_X * N_Z
N_BLK = 32
HALF = N_Z // 2
OWN_SLOT = 0
GROUP = 4
N_RELAY = 12
EARLY = 1
SCALE = math.log2(math.e) / math.sqrt(HEAD_DIM)


def peer(uly, slot, sign):
    x, z = uly // N_Z, lax.rem(uly, N_Z)
    half, place = z // HALF, lax.rem(z, HALF)
    near, turn = 1 - slot // 12, lax.rem(slot, 12)
    dz, dx = turn // N_X, lax.rem(turn, N_X)
    to_half = jnp.where(near == 1, half, 1 - half)
    to_place = lax.rem(place + sign * dz + HALF, HALF)
    to_x = lax.rem(x + sign * dx + N_X, N_X)
    return to_x * N_Z + to_half * HALF + to_place


def kernel(
    x_ref, o_ref, top_ref, total_ref, queries, own, prev, stage,
    loc_sem, q_send, q_recv, kv_send, kv_recv, f_send, f_recv, a_send, a_recv, b_send, ready,
):
    blk, uly = lax.axis_index("blk"), lax.axis_index("uly")
    zhi, y, core = blk // (2 * N_Y), lax.rem(blk // 2, N_Y), lax.rem(blk, 2)
    tokens = x_ref.shape[1]
    following, preceding = lax.rem(blk + 1, N_BLK), lax.rem(blk + N_BLK - 1, N_BLK)
    last = jnp.logical_and(y == N_Y - 1, core == 1)
    first = jnp.logical_and(y == 0, core == 0)
    relay = jnp.logical_and(y >= 1, y <= N_RELAY // 2)
    lower = zhi == 0
    relay_slot = 2 * (y - 1) + core + 0

    def block_at(zhi_, y_, core_):
        return (zhi_ * N_Y + y_) * 2 + core_

    def relay_at(zhi_, c):
        return block_at(zhi_, 1 + c // 2, lax.rem(c, 2))

    wrap_source = block_at(zhi, N_Y - 1, 1)
    wrap_target = block_at(1 - zhi, 0, 0)
    wrap_origin = block_at(1 - zhi, N_Y - 1, 1)

    barrier = pltpu.get_barrier_semaphore()

    def greet(b, u):
        pl.semaphore_signal(barrier, inc=1, device_id=(b, u), device_id_type=MESH)

    @pl.loop(1, N_ULY)
    def _(k):
        greet(blk, lax.rem(uly + k, N_ULY))

    @pl.when(jnp.logical_not(first))
    def _():
        greet(preceding, uly)

    @pl.when(relay)
    def _():
        greet(wrap_source, uly)

    @pl.when(jnp.logical_and(relay, lower))
    def _():
        greet(wrap_target, peer(uly, relay_slot, 1))

    @pl.when(jnp.logical_and(last, lower))
    def _():
        @pl.loop(0, N_RELAY)
        def _(c):
            greet(wrap_target, peer(uly, c + 12, 1))

    @pl.when(jnp.logical_and(first, lower))
    def _():
        @pl.loop(0, N_RELAY)
        def _(c):
            greet(wrap_origin, peer(uly, c + 12, -1))
            greet(relay_at(1 - zhi, c), peer(uly, (c + 0), -1))

    extra = jnp.where(
        lower, 0, jnp.where(first, N_ULY, jnp.where(last, N_RELAY, jnp.where(relay, 1, 0)))
    )
    pl.semaphore_wait(barrier, N_ULY - 1 + jnp.where(last, N_RELAY, 1) + extra)

    @pl.when(jnp.logical_and(first, jnp.logical_not(lower)))
    def _():
        @pl.loop(0, N_RELAY)
        def _(c):
            pl.semaphore_signal(
                ready, inc=1, device_id=(wrap_origin, peer(uly, c + 12, -1)), device_id_type=MESH
            )
            pl.semaphore_signal(
                ready, inc=1, device_id=(relay_at(1 - zhi, c), peer(uly, (c + 0), -1)),
                device_id_type=MESH,
            )

    def rows(s):
        return pl.ds(pl.multiple_of(s * tokens, tokens), tokens)

    def head(u):
        return pl.ds(pl.multiple_of(u * HEAD_DIM, HEAD_DIM), HEAD_DIM)

    remote = functools.partial(pltpu.make_async_remote_copy, device_id_type=MESH)

    def send_q(j):
        to = peer(uly, j, 1)
        return remote(
            x_ref.at[0, :, head(to)], queries.at[rows(uly)], q_send.at[j], q_recv.at[j],
            device_id=(blk, to),
        )

    def send_kv(j):
        to = peer(uly, j, 1)
        return remote(
            x_ref.at[1:3, :, head(to)], own.at[:, rows(j)], kv_send.at[j], kv_recv.at[j],
            device_id=(blk, to),
        )

    def forward(j):
        return remote(
            own.at[:, rows(j)], prev.at[:, rows(j)], f_send.at[j], f_recv.at[j],
            device_id=(following, uly),
        )

    def spread(c):
        return remote(
            x_ref.at[1:3, :, head(peer(uly, (c + 0), 1))], stage, a_send.at[c], a_recv,
            device_id=(relay_at(zhi, c), uly),
        )

    def cross_staged():
        return remote(
            stage, prev.at[:, rows(relay_slot)], b_send.at[0], f_recv.at[relay_slot],
            device_id=(wrap_target, peer(uly, relay_slot, 1)),
        )

    def cross_direct(c):
        to = peer(uly, c + 12, 1)
        return remote(
            x_ref.at[1:3, :, head(to)], prev.at[:, rows((c + 12))], b_send.at[c], f_recv.at[c + 12],
            device_id=(wrap_target, to),
        )

    own_q = pltpu.make_async_copy(x_ref.at[0, :, head(uly)], queries.at[rows(uly)], loc_sem.at[0])
    own_kv = pltpu.make_async_copy(
        x_ref.at[1:3, :, head(uly)], own.at[:, rows(OWN_SLOT)], loc_sem.at[1]
    )
    own_q.start()
    own_kv.start()

    @pl.when(last)
    def _():
        @pl.loop(0, N_RELAY)
        def _(c):
            spread(c).start()

    @pl.when(jnp.logical_and(last, jnp.logical_not(lower)))
    def _():
        @pl.loop(0, N_RELAY)
        def _(c):
            cross_direct(c).start()

    @pl.loop(0, N_ULY)
    def _(i):
        j = lax.rem(i + N_ULY // 2, N_ULY)

        @pl.when(j != OWN_SLOT)
        def _():
            send_q(j).start()

    @pl.loop(0, EARLY)
    def _(j):
        @pl.when(j != OWN_SLOT)
        def _():
            send_kv(j).start()

    @pl.when(relay)
    def _():
        @pl.when(lower)
        def _():
            pl.semaphore_wait(ready, 1)

        spread(0).wait_recv()
        cross_staged().start()

    @pl.when(jnp.logical_and(last, lower))
    def _():
        pl.semaphore_wait(ready, N_RELAY)

    @pl.loop(EARLY, N_ULY)
    def _(j):
        @pl.when(jnp.logical_and(last, lower))
        def _():
            @pl.when(j < EARLY + N_RELAY)
            def _():
                cross_direct(j - EARLY).start()

        @pl.when(j != OWN_SLOT)
        def _():
            send_kv(j).start()

    own_q.wait()
    own_kv.wait()

    @pl.when(jnp.logical_not(last))
    def _():
        forward(OWN_SLOT).start()

    @pl.loop(0, N_ULY)
    def _(j):
        @pl.when(j != OWN_SLOT)
        def _():
            send_q(j).wait_recv()

    def arrive(g):
        @pl.loop(0, GROUP)
        def _(i):
            j = g * GROUP + i

            @pl.when(j != OWN_SLOT)
            def _():
                send_kv(j).wait_recv()

                @pl.when(jnp.logical_not(last))
                def _():
                    forward(j).start()

    def arrive_prev(g):
        @pl.loop(0, GROUP)
        def _(i):
            forward(g * GROUP + i).wait_recv()

    wide = GROUP * tokens

    def attend(held, g, start):
        span = pl.ds(pl.multiple_of(g * wide, wide), wide)
        scores = lax.dot_general(
            queries[...], held[0, span, :], (((1,), (1,)), ((), ())),
            preferred_element_type=jnp.float32,
        )
        high = jnp.max(scores, axis=1, keepdims=True) * SCALE
        if start:
            new_top = jnp.broadcast_to(high, top_ref.shape)
        else:
            old_top = top_ref[...]
            new_top = jnp.maximum(old_top, high)
            factor = jnp.exp2(old_top - new_top)
        copies = wide // HEAD_DIM
        weights = jnp.exp2(scores * SCALE - jnp.concatenate([new_top] * copies, axis=1))
        part = weights[:, :HEAD_DIM]
        for a in range(1, copies):
            part = part + weights[:, a * HEAD_DIM : (a + 1) * HEAD_DIM]
        product = jnp.dot(
            weights.astype(jnp.bfloat16), held[1, span, :], preferred_element_type=jnp.float32
        )
        top_ref[...] = new_top
        total_ref[...] = part if start else total_ref[...] * factor + part
        o_ref[...] = product if start else o_ref[...] * factor + product

    groups = N_ULY // GROUP
    lag = 2
    arrive(0)
    attend(own, 0, True)

    def take_own(g):
        arrive(g)
        attend(own, g, False)

    def take_prev(g):
        arrive_prev(g)
        attend(prev, g, False)

    pl.loop(1, lag)(take_own)

    @pl.loop(lag, groups - 1)
    def _(g):
        take_own(g)
        take_prev(g - lag)

    take_prev(groups - 1 - lag)
    take_own(groups - 1)
    pl.loop(groups - lag, groups)(take_prev)

    @pl.loop(0, N_ULY)
    def _(j):
        @pl.when(j != OWN_SLOT)
        def _():
            send_q(j).wait_send()
            send_kv(j).wait_send()

        @pl.when(jnp.logical_not(last))
        def _():
            forward(j).wait_send()

    @pl.when(last)
    def _():
        @pl.loop(0, N_RELAY)
        def _(c):
            spread(c).wait_send()
            cross_direct(c).wait_send()

    @pl.when(relay)
    def _():
        cross_staged().wait_send()


def finish(a_ref, top_ref, total_ref, o_ref, l_ref):
    diagonal = lax.broadcasted_iota(jnp.int32, (HEAD_DIM, HEAD_DIM), 0) == lax.broadcasted_iota(
        jnp.int32, (HEAD_DIM, HEAD_DIM), 1
    )
    for i in range(o_ref.shape[0] // HEAD_DIM):
        span = pl.ds(i * HEAD_DIM, HEAD_DIM)
        total = jnp.sum(total_ref[span, :], axis=1, keepdims=True)
        o_ref[span, :] = a_ref[span, :] / total
        logs = top_ref[span, :] * math.log(2) + jnp.log(total)
        l_ref[:, span] = jnp.sum(jnp.where(diagonal, logs, 0.0), axis=0, keepdims=True)


def shards(qkv):
    tokens, _, width = qkv.shape
    block_len = tokens * N_ULY
    dma = pltpu.SemaphoreType.DMA
    in_vmem = pl.BlockSpec(memory_space=pltpu.VMEM)
    rows = jax.ShapeDtypeStruct((block_len, HEAD_DIM), jnp.float32)
    parts = pl.pallas_call(
        kernel,
        name="regroup_attend",
        out_shape=(rows, rows, rows),
        in_specs=[pl.BlockSpec(memory_space=pltpu.HBM)],
        out_specs=(in_vmem, in_vmem, in_vmem),
        scratch_shapes=[
            pltpu.VMEM((block_len, HEAD_DIM), jnp.bfloat16),
            pltpu.VMEM((2, block_len, HEAD_DIM), jnp.bfloat16),
            pltpu.VMEM((2, block_len, HEAD_DIM), jnp.bfloat16),
            pltpu.VMEM((2, tokens, HEAD_DIM), jnp.bfloat16),
            dma((2,)),
            dma((N_ULY,)), dma((N_ULY,)), dma((N_ULY,)), dma((N_ULY,)),
            dma((N_ULY,)), dma((N_ULY,)), dma((N_RELAY,)), dma, dma((N_RELAY,)),
            pltpu.SemaphoreType.REGULAR,
        ],
        compiler_params=pltpu.CompilerParams(
            collective_id=0, has_side_effects=True, vmem_limit_bytes=48 << 20
        ),
        cost_estimate=pl.CostEstimate(
            flops=8 * block_len * block_len * HEAD_DIM,
            bytes_accessed=10 * block_len * HEAD_DIM,
            transcendentals=2 * block_len * block_len,
        ),
    )(pltpu.with_memory_space_constraint(jnp.transpose(qkv, (1, 0, 2)), pltpu.HBM))
    return pl.pallas_call(
        finish,
        name="finish",
        out_shape=(rows, jax.ShapeDtypeStruct((1, block_len), jnp.float32)),
        in_specs=[in_vmem] * 3,
        out_specs=(in_vmem, in_vmem),
        compiler_params=pltpu.CompilerParams(vmem_limit_bytes=8 << 20),
    )(*parts)


def solution(mesh):
    return jax.shard_map(
        shards,
        mesh=mesh,
        in_specs=(P(("blk", "uly"), None, None),),
        out_specs=(P("blk", "uly"), P("uly", "blk")),
        check_vma=False,
    )
```
